32 devices in a mesh: group: 2 (over x), cell: 16 (over z, y, core).
Axes of the slice: x: 2, y: 2, z: 4, core: 2. Of those that a mesh axis runs over, the one named last changes fastest.
Arguments:
- adjoint_seed: float32 [32, 5, 16384], P('group', None, 'cell'), parts along dimension 0, may hold values from -6 to 6
- inv_blocks: bfloat16 [32, 5, 5, 16384], P('group', None, None, 'cell'), parts along dimension 0
- flux_jacobians: float32 [2, 32, 5, 5], P(None, 'group'), parts along dimension 1, may hold values from -1.5 to 1.5
- modal_shapes: float32 [20, 5, 16384], P(None, None, 'cell'), may hold values from -0.01953125 to 0.01953125
- modal_gain: float32 [40], P('group'), parts along dimension 0, may hold values from 0.05 to 0.3
- face_cells: int32 [2, 49152], P(None, 'cell'), may hold values from 0 to 1279, as said below
- face_weights: float32 [49152], P('cell'), may hold values from 0.4 to 1
- colours: int32 [16384], P('cell'), may hold values from 0 to 1
- send_cells: int32 [2, 2048], P(None, 'cell'), may hold values from 0 to 1023, as said below
Outputs:
- adjoint_state: float32 [32, 5, 16384], P('group', None, 'cell'), parts along dimension 0
- modal_partials: float32 [32, 20], P('group'), parts along dimension 0
The draws below stay inside these ranges and needn't reach their ends.
There are 2 independent parts, one for each index of `group`. The reference program is written for one: setup_inputs(seed, part) draws one part's arguments, and reference() takes and returns one part's arrays. A program takes and returns all parts, laid end to end along the dimension named above; an argument that names none is the same for every part. Nothing has to cross between parts.
Inputs may be any that keep to these rules, and one draw needn't show every extreme that they name: `face_cells`: each face's left cell is a local cell or a lower ghost (from 1024 to 1151); its right cell is a local cell or an upper ghost (from 1152 on). `send_cells`: within a partition the 256 listed cells are distinct local cells.
All inputs are finite; a program needn't handle non-finite values.
Results may differ from the reference program's by a relative error of at most 0.0003.
Values sent between devices are 32-bit elements; how exact they have to be, the bound alone decides.
A program may use at most 64 MiB of HBM per device.

```python
import math
import jax
import jax.numpy as jnp
from jax import lax

NI = 16
NV = 5
MODES = 20
ITERS = 4
CELLS_DEV = 1024
HALO = 128
FACES_DEV = 3072
CELLS = 16384
FACES = 49152
HALOS = 2048
N_CELL = 16


def draw_inv_blocks(key, part):
    first, second = jax.random.split(jax.random.fold_in(key, 11))
    diagonal = jnp.exp(jax.random.uniform(first, (NI, NV, CELLS), jnp.float32, jnp.log(0.25), jnp.log(0.6)))
    offdiag = 0.1 * jax.random.normal(second, (NI, NV, NV, CELLS), jnp.float32)
    unit = jnp.eye(NV, dtype=jnp.float32)[None, :, :, None]
    blocks = offdiag * (1.0 - unit) + diagonal[:, :, None, :] * unit
    return blocks.astype(jnp.bfloat16)


def draw_face_cells(key, part):
    count = FACES // FACES_DEV
    keys = jax.random.split(jax.random.fold_in(key, 23), 4)
    owner = jax.random.randint(keys[0], (count, FACES_DEV), 0, CELLS_DEV)
    step = jax.random.randint(keys[1], (count, FACES_DEV), 1, 3 * HALO)
    reach = owner + step
    right_cells = jnp.where(reach < CELLS_DEV, reach, CELLS_DEV + HALO + (reach - CELLS_DEV) % HALO)
    lowered = jax.random.randint(keys[2], (count, FACES_DEV), 0, 8) == 0
    left_cells = jnp.where(lowered, CELLS_DEV + jax.random.randint(keys[3], (count, FACES_DEV), 0, HALO), owner)
    return jnp.stack([left_cells, right_cells]).reshape(2, FACES).astype(jnp.int32)


def draw_send_cells(key, part):
    count = HALOS // HALO
    keys = jax.random.split(jax.random.fold_in(key, 37), count)
    chosen = jax.vmap(lambda single: jax.random.permutation(single, CELLS_DEV)[:2 * HALO])(keys)
    chosen = chosen.reshape(count, 2, HALO)
    return jnp.transpose(chosen, (1, 0, 2)).reshape(2, HALOS).astype(jnp.int32)


def with_ends(drawn, stream_key, low, largest):
    longest = drawn.shape.index(max(drawn.shape))
    spots = []
    for shift in (0, 1):
        where = [jax.random.randint(jax.random.fold_in(stream_key, axis), (), 0, length) for axis, length in enumerate(drawn.shape)]
        where[longest] = (where[longest] + shift) % drawn.shape[longest]
        spots.append(tuple(where))
    return drawn.at[spots[0]].set(low).at[spots[1]].set(largest)


def block_scale(key, extent, shards, low, largest):
    loudness, own = 1.0, jax.random.fold_in(key, 6)
    for dim, blocks in shards:
        steps = jnp.exp(jax.random.uniform(jax.random.fold_in(own, dim), (blocks,), jnp.float32, low / len(shards), largest / len(shards)))
        loudness = loudness * jnp.repeat(steps, extent[dim] // blocks).reshape([-1 if axis == dim else 1 for axis in range(len(extent))])
    return loudness


def gaussian(stream_key, shape, scale, bound, pieces=(), kind=jnp.bfloat16):
    values = jax.random.normal(stream_key, shape, jnp.float32) * scale
    if len(pieces) > 0:
        values = block_scale(stream_key, shape, pieces, -0.22, 0.18) * values
    return jnp.clip(values, min=-bound, max=bound).astype(kind)


def setup_inputs(seed: int = 0, part: int = 0) -> dict:
    key_list = jax.random.split(jax.random.key(seed), 10)
    part_keys = jax.random.split(jax.random.fold_in(key_list[9], part), 10)
    return {
        "adjoint_seed": gaussian(part_keys[0], (NI, NV, CELLS), 1.0, 6.0, ((2, 16),), jnp.float32),
        "inv_blocks": draw_inv_blocks(jax.random.fold_in(jax.random.fold_in(key_list[9], part), 71), part),
        "flux_jacobians": gaussian(part_keys[2], (2, NI, NV, NV), 0.25, 1.5, (), jnp.float32),
        "modal_shapes": gaussian(key_list[3], (MODES, NV, CELLS), (NV * CELLS) ** -0.5, 0.01953125, ((2, 16),), jnp.float32),
        "modal_gain": jnp.clip(jnp.exp(jax.random.uniform(part_keys[4], (MODES,), jnp.float32, math.log(0.05), math.log(0.3))), 0.05, 0.3),
        "face_cells": draw_face_cells(jax.random.fold_in(key_list[9], 71), part),
        "face_weights": jnp.clip(0.4 + 0.6 * jax.random.uniform(key_list[6], (FACES,), jnp.float32) ** block_scale(key_list[6], (FACES,), ((0, 16),), -0.2, 0.2), 0.4, 1.0),
        "colours": with_ends(jax.random.randint(key_list[7], (CELLS,), 0, 2), jax.random.fold_in(key_list[7], 1), 0, 1).astype(jnp.int32),
        "send_cells": draw_send_cells(jax.random.fold_in(key_list[9], 71), part),
    }


frequency = 0.04


def spectral_matrix(count):
    index = jnp.arange(count)
    apart = index[:, None] - index[None, :]
    angle = math.pi * apart.astype(jnp.float32) / count
    parity = jnp.where(apart % 2 == 0, 1.0, -1.0).astype(jnp.float32)
    safe_sin = jnp.where(apart == 0, 1.0, jnp.sin(angle))
    return jnp.where(apart == 0, 0.0, 0.5 * parity * jnp.cos(angle) / safe_sin).astype(jnp.float32)


def off_product(extended, jacobians, faces, weights, owned):
    left_cells = faces[0]
    right_cells = faces[1]
    from_left = jnp.einsum('nvw,nvc->nwc', jacobians[0], extended, precision=lax.Precision.HIGHEST)
    from_right = jnp.einsum('nvw,nvc->nwc', jacobians[1], extended, precision=lax.Precision.HIGHEST)
    total = jnp.zeros_like(extended)
    total = total.at[:, :, right_cells].add(weights * jnp.take(from_left, left_cells, axis=2))
    total = total.at[:, :, left_cells].add(weights * jnp.take(from_right, right_cells, axis=2))
    return total[:, :, :owned]


def reference(adjoint_seed, inv_blocks, flux_jacobians, modal_shapes, modal_gain, face_cells, face_weights, colours, send_cells):
    parts = N_CELL

    def split(array):
        shaped = array.reshape(array.shape[:-1] + (parts, array.shape[-1] // parts))
        return jnp.moveaxis(shaped, -2, 0)

    seed_p = split(adjoint_seed)
    inv_p = split(inv_blocks).astype(jnp.float32)
    shapes_p = split(modal_shapes)
    faces_p = split(face_cells)
    weights_p = split(face_weights)
    colour_p = split(colours)
    sends_p = split(send_cells)
    spectral = spectral_matrix(NI)
    owned = CELLS_DEV

    def modal(state):
        return jnp.einsum('pnvc,pmvc->nm', state, shapes_p, precision=lax.Precision.HIGHEST)

    state = jnp.zeros_like(seed_p)
    for sweep in range(ITERS):
        lam = modal(state) * modal_gain[None, :]
        base = seed_p + jnp.einsum('nm,pmvc->pnvc', lam, shapes_p, precision=lax.Precision.HIGHEST)
        sent = jax.vmap(lambda field, lists: jnp.take(field, lists, axis=2))(state, sends_p)
        from_lower = jnp.roll(sent[:, :, :, 1, :], 1, axis=0)
        from_upper = jnp.roll(sent[:, :, :, 0, :], -1, axis=0)
        ghosts = jnp.concatenate([from_lower, from_upper], axis=-1)
        for colour in range(2):
            extended = jnp.concatenate([state, ghosts], axis=-1)
            coupled = jax.vmap(off_product, (0, None, 0, 0, None))(extended, flux_jacobians, faces_p, weights_p, owned)
            spectral_term = frequency * jnp.einsum('mn,pmvc->pnvc', spectral, state, precision=lax.Precision.HIGHEST)
            resid = base - coupled - spectral_term
            updated = jnp.sum(inv_p * resid[:, :, :, None, :], axis=2)
            state = jnp.where(colour_p[:, None, None, :] == colour, updated, state)
    partials = modal(state)
    merged = jnp.moveaxis(state, 0, -2).reshape(adjoint_seed.shape)
    return merged, partials
```

```python
import functools
import math

import jax
import jax.numpy as jnp
from jax import lax
from jax.experimental import pallas as pl
from jax.experimental.pallas import tpu as pltpu
from jax.sharding import PartitionSpec as P

ITERS = 4
FREQUENCY = 0.04
F32 = jnp.float32
BF16 = jnp.bfloat16
MODE_ROWS = 32


def spectral_matrix(count):
    index = jnp.arange(count)
    apart = index[:, None] - index[None, :]
    angle = math.pi * apart.astype(F32) / count
    parity = jnp.where(apart % 2 == 0, 1.0, -1.0).astype(F32)
    safe_sin = jnp.where(apart == 0, 1.0, jnp.sin(angle))
    return jnp.where(apart == 0, 0.0, 0.5 * parity * jnp.cos(angle) / safe_sin)


def split(value):
    high = value.astype(BF16)
    return high, (value - high.astype(F32)).astype(BF16)


def mm(left, right):
    return jnp.dot(left, right, preferred_element_type=F32)


def mm_nt(left, right):
    return lax.dot_general(left, right, (((1,), (1,)), ((), ())), preferred_element_type=F32)


def kernel(
    n,
    seed_ref,
    inv_ref,
    w_in_ref,
    shapes_ref,
    gain_ref,
    faces_ref,
    g_ref,
    col_ref,
    send_ref,
    out_ref,
    part_ref,
    w_ref,
    left_hot,
    m_high,
    m_low,
    mg_high,
    mg_low,
    p_ref,
    sel_ref,
    x_ref,
    z_ref,
    base_ref,
    ab_ref,
    q_all,
    ghost_out,
    ghost_in,
    q_send,
    q_recv,
    g_send,
    g_recv,
):
    count, nvar, owned = seed_ref.shape
    modes = shapes_ref.shape[0]
    rows = count * nvar
    halo = send_ref.shape[1]
    nfaces = g_ref.shape[1]
    me = lax.axis_index("cell")
    peers = [lax.rem(me + d, n) for d in range(n)]

    barrier = pltpu.get_barrier_semaphore()
    for d in range(1, n):
        pl.semaphore_signal(barrier, inc=1, device_id={"cell": peers[d]}, device_id_type=pl.DeviceIdType.MESH)

    left = faces_ref[0:1, :]
    right = faces_ref[1:2, :]
    g_high, g_low = split(g_ref[...])
    g_high = g_high.astype(F32)
    g_low = g_low.astype(F32)
    step = 128
    tall = owned + halo

    @pl.loop(0, tall // step)
    def _(t):
        at = pl.multiple_of(t * step, step)
        hit = left == lax.broadcasted_iota(jnp.int32, (step, nfaces), 0) + at
        left_hot[0, pl.ds(at, step), :] = jnp.where(hit, g_high, 0.0).astype(BF16)
        left_hot[1, pl.ds(at, step), :] = jnp.where(hit, g_low, 0.0).astype(BF16)

    wide = 256
    tall_step = tall // 3

    @pl.loop(0, owned // wide)
    def _(t):
        at = pl.multiple_of(t * wide, wide)
        hit = right == lax.broadcasted_iota(jnp.int32, (wide, nfaces), 0) + at
        hot = jnp.where(hit, 1.0, 0.0).astype(BF16)
        for part in range(3):
            r0 = part * tall_step
            block = mm_nt(left_hot[0, r0 : r0 + tall_step, :], hot) + mm_nt(left_hot[1, r0 : r0 + tall_step, :], hot)
            high, low = split(block)
            here = min(r0 + tall_step, owned) - r0
            m_high[r0 : r0 + here, pl.ds(at, wide)] = high[:here]
            m_low[r0 : r0 + here, pl.ds(at, wide)] = low[:here]
            if here < tall_step:
                mg_high[0:halo, pl.ds(at, wide)] = high[here:]
                mg_low[0:halo, pl.ds(at, wide)] = low[here:]

    hit = right == lax.broadcasted_iota(jnp.int32, (halo, nfaces), 0) + (owned + halo)
    upper_high = jnp.where(hit, g_high, 0.0).astype(BF16)
    upper_low = jnp.where(hit, g_low, 0.0).astype(BF16)
    upper_hot = jnp.concatenate([upper_high, upper_low], axis=0)

    @pl.loop(0, owned // wide)
    def _(t):
        at = pl.multiple_of(t * wide, wide)
        hit = left == lax.broadcasted_iota(jnp.int32, (wide, nfaces), 0) + at
        hot = jnp.where(hit, 1.0, 0.0).astype(BF16)
        block = mm_nt(upper_hot, hot)
        high, low = split(block[:halo] + block[halo:])
        mg_high[halo:, pl.ds(at, wide)] = high
        mg_low[halo:, pl.ds(at, wide)] = low

    w_high, w_low = split(w_in_ref[...])
    lane = lax.broadcasted_iota(jnp.int32, (3 * rows, 3 * rows), 1)
    w_ref[...] = jnp.where(lane < 2 * rows, w_high.astype(F32), w_low.astype(F32)).astype(BF16)
    send_row = jnp.concatenate([send_ref[0:1, :], send_ref[1:2, :]], axis=1)
    sel_ref[...] = jnp.where(
        send_row == lax.broadcasted_iota(jnp.int32, (owned, 2 * halo), 0), 1.0, 0.0
    ).astype(BF16)
    for v in range(nvar):
        shape_v = shapes_ref[:, v, :]
        shape_v = jnp.concatenate([shape_v, jnp.zeros((MODE_ROWS - modes, owned), F32)], axis=0)
        high, low = split(shape_v)
        p_ref[v, 0:MODE_ROWS, :] = high
        p_ref[v, MODE_ROWS:, :] = low
        z_ref[v * count : (v + 1) * count, :] = seed_ref[:, v, :]
    colours = col_ref[...]

    def update(colour):
        mask = colours == colour
        for w in range(nvar):
            spot = slice(w * count, (w + 1) * count)
            total = inv_ref[0, w].astype(F32) * z_ref[0:count, :]
            for v in range(1, nvar):
                total = total + inv_ref[v, w].astype(F32) * z_ref[v * count : (v + 1) * count, :]
            x_ref[spot, :] = jnp.where(mask, total, x_ref[spot, :])

    def coupling():
        high, low = split(x_ref[...])
        both = mm(w_ref[...], jnp.concatenate([high, low, high], axis=0))
        a_high, a_low = split(both[:rows])
        b_high, b_low = split(both[rows : 2 * rows])
        ab_ref[0, 0:rows, :] = a_high
        ab_ref[0, rows:, :] = a_low
        ab_ref[1, 0:rows, :] = b_high
        ab_ref[1, rows:, :] = b_low
        z_ref[...] = both[2 * rows :]

        @pl.loop(0, owned // wide)
        def _(t):
            at = pl.multiple_of(t * wide, wide)
            cols = pl.ds(at, wide)
            one = mm(ab_ref[0], m_high[:, cols]) + mm_nt(ab_ref[1], m_high[cols, :])
            two = mm(ab_ref[0, 0:rows, :], m_low[:, cols]) + mm_nt(ab_ref[1, 0:rows, :], m_low[cols, :])
            z_ref[:, cols] = z_ref[:, cols] + (one[:rows] + one[rows:] + two)

    def modal_copies(turn):
        return [
            pltpu.make_async_remote_copy(
                src_ref=q_all.at[turn, me],
                dst_ref=q_all.at[turn, me],
                send_sem=q_send.at[turn, d],
                recv_sem=q_recv.at[turn, d],
                device_id={"cell": peers[d]},
                device_id_type=pl.DeviceIdType.MESH,
            )
            for d in range(1, n)
        ]

    def ghost_copies(turn):
        return [
            pltpu.make_async_remote_copy(
                src_ref=ghost_out.at[turn, way],
                dst_ref=ghost_in.at[turn, 1 - way],
                send_sem=g_send.at[turn, way],
                recv_sem=g_recv.at[turn, way],
                device_id={"cell": peers[n - 1 if way == 0 else 1]},
                device_id_type=pl.DeviceIdType.MESH,
            )
            for way in range(2)
        ]

    def start_exchange(turn):
        high, low = split(x_ref[...])
        copies = []
        if turn < ITERS - 1:
            picked = mm(jnp.concatenate([high, low], axis=0), sel_ref[...])
            picked = picked[:rows] + picked[rows:]
            ghost_out[turn, 0] = picked[:, :halo]
            ghost_out[turn, 1] = picked[:, halo:]
            copies = ghost_copies(turn)
            if turn == 0:
                pl.semaphore_wait(barrier, n - 1)
            for copy in copies:
                copy.start()
        gram = jnp.zeros((2 * count, 2 * MODE_ROWS), F32)
        for v in range(nvar):
            spot = slice(v * count, (v + 1) * count)
            gram = gram + mm_nt(jnp.concatenate([high[spot], low[spot]], axis=0), p_ref[v])
        gram = gram[:count] + gram[count:]
        part = gram[:, :MODE_ROWS] + gram[:, MODE_ROWS:]
        q_all[turn, me] = jnp.concatenate([part, jnp.zeros((count, 128 - MODE_ROWS), F32)], axis=1)
        modal = modal_copies(turn)
        for copy in modal:
            copy.start()
        return copies + modal

    def modal_sum(turn):
        total = q_all[turn, 0]
        for d in range(1, n):
            total = total + q_all[turn, d]
        return total

    x_ref[...] = jnp.zeros((rows, owned), F32)
    update(0)
    coupling()
    for v in range(nvar):
        spot = slice(v * count, (v + 1) * count)
        z_ref[spot, :] = seed_ref[:, v, :] - z_ref[spot, :]
    update(1)
    copies = start_exchange(0)
    for sweep in range(1, ITERS):
        coupling()
        for copy in copies:
            copy.wait()
        low_part = ghost_in[sweep - 1, 0]
        up_part = ghost_in[sweep - 1, 1]
        high, low = split(jnp.concatenate([low_part, up_part], axis=1))
        both = mm(w_ref[0 : 2 * rows, :], jnp.concatenate([high, low, high], axis=0))
        ghost_ab = jnp.concatenate([both[:rows, :halo], both[rows:, halo:]], axis=1)
        high, low = split(ghost_ab)
        term = mm(jnp.concatenate([high, low], axis=0), mg_high[...])
        term = term[:rows] + term[rows:] + mm(high, mg_low[...])
        lam = modal_sum(sweep - 1)[:, :MODE_ROWS] * gain_ref[...]
        lam_high, lam_low = split(lam)
        lam_both = jnp.concatenate([lam_high, lam_low], axis=0)
        for v in range(nvar):
            spot = slice(v * count, (v + 1) * count)
            lift = mm(lam_both, p_ref[v, 0:MODE_ROWS, :])
            lift = lift[:count] + lift[count:] + mm(lam_high, p_ref[v, MODE_ROWS:, :])
            base = seed_ref[:, v, :] + lift - term[spot]
            base_ref[spot, :] = base
            z_ref[spot, :] = base - z_ref[spot, :]
        update(0)
        coupling()
        z_ref[...] = base_ref[...] - z_ref[...]
        update(1)
        copies = start_exchange(sweep)
    for v in range(nvar):
        out_ref[:, v, :] = x_ref[v * count : (v + 1) * count, :]
    for copy in copies:
        copy.wait()
    part_ref[...] = modal_sum(ITERS - 1)[:, :modes]


def local(
    adjoint_seed,
    inv_blocks,
    flux_jacobians,
    modal_shapes,
    modal_gain,
    face_cells,
    face_weights,
    colours,
    send_cells,
):
    n = lax.axis_size("cell")
    count, nvar, owned = adjoint_seed.shape
    modes = modal_shapes.shape[0]
    rows = count * nvar
    halo = send_cells.shape[1]
    nfaces = face_weights.shape[0]
    eye_inst = jnp.eye(count, dtype=F32)
    eye_var = jnp.eye(nvar, dtype=F32)
    left_matrix = (
        jnp.transpose(flux_jacobians[0], (2, 0, 1))[:, :, :, None] * eye_inst[None, :, None, :]
    ).reshape(rows, rows)
    right_matrix = (
        jnp.transpose(flux_jacobians[1], (2, 0, 1))[:, :, :, None] * eye_inst[None, :, None, :]
    ).reshape(rows, rows)
    spectral = FREQUENCY * spectral_matrix(count)
    spectral_rows = (eye_var[:, None, :, None] * spectral.T[None, :, None, :]).reshape(rows, rows)
    stacked = jnp.concatenate([left_matrix, right_matrix, spectral_rows], axis=0)
    weights = jnp.concatenate([stacked, stacked, stacked], axis=1)
    inverse = jnp.transpose(inv_blocks, (1, 2, 0, 3))
    gain = jnp.concatenate([modal_gain, jnp.zeros((MODE_ROWS - modes,), F32)])[None, :]
    vmem = pl.BlockSpec(memory_space=pltpu.VMEM)
    tall = owned + halo
    turns = ITERS
    out, part = pl.pallas_call(
        functools.partial(kernel, n),
        out_shape=(
            jax.ShapeDtypeStruct((count, nvar, owned), F32),
            jax.ShapeDtypeStruct((count, modes), F32),
        ),
        in_specs=[vmem] * 9,
        out_specs=(vmem, vmem),
        scratch_shapes=[
            pltpu.VMEM((3 * rows, 3 * rows), BF16),
            pltpu.VMEM((2, tall, nfaces), BF16),
            pltpu.VMEM((owned, owned), BF16),
            pltpu.VMEM((owned, owned), BF16),
            pltpu.VMEM((2 * halo, owned), BF16),
            pltpu.VMEM((2 * halo, owned), BF16),
            pltpu.VMEM((nvar, 2 * MODE_ROWS, owned), BF16),
            pltpu.VMEM((owned, 2 * halo), BF16),
            pltpu.VMEM((rows, owned), F32),
            pltpu.VMEM((rows, owned), F32),
            pltpu.VMEM((rows, owned), F32),
            pltpu.VMEM((2, 2 * rows, owned), BF16),
            pltpu.VMEM((turns, n, count, 128), F32),
            pltpu.VMEM((turns - 1, 2, rows, halo), F32),
            pltpu.VMEM((turns - 1, 2, rows, halo), F32),
            pltpu.SemaphoreType.DMA((turns, n)),
            pltpu.SemaphoreType.DMA((turns, n)),
            pltpu.SemaphoreType.DMA((turns - 1, 2)),
            pltpu.SemaphoreType.DMA((turns - 1, 2)),
        ],
        compiler_params=pltpu.CompilerParams(
            collective_id=0, has_side_effects=True, vmem_limit_bytes=56 * 1024 * 1024
        ),
    )(
        adjoint_seed,
        inverse,
        weights,
        modal_shapes,
        gain,
        face_cells,
        face_weights[None, :],
        colours[None, :],
        send_cells,
    )
    return out, part


def solution(mesh):
    return jax.shard_map(
        local,
        mesh=mesh,
        in_specs=(
            P("group", None, "cell"),
            P("group", None, None, "cell"),
            P(None, "group", None, None),
            P(None, None, "cell"),
            P("group"),
            P(None, "cell"),
            P("cell"),
            P("cell"),
            P(None, "cell"),
        ),
        out_specs=(P("group", None, "cell"), P("group", None)),
        check_vma=False,
    )
```

```python
import functools
import math

import jax
import jax.numpy as jnp
from jax import lax
from jax.experimental import pallas as pl
from jax.experimental.pallas import tpu as pltpu
from jax.sharding import PartitionSpec as P

ITERS = 4
FREQUENCY = 0.04
F32 = jnp.float32
BF16 = jnp.bfloat16
MODE_ROWS = 32


def spectral_matrix(count):
    index = jnp.arange(count)
    apart = index[:, None] - index[None, :]
    angle = math.pi * apart.astype(F32) / count
    parity = jnp.where(apart % 2 == 0, 1.0, -1.0).astype(F32)
    safe_sin = jnp.where(apart == 0, 1.0, jnp.sin(angle))
    return jnp.where(apart == 0, 0.0, 0.5 * parity * jnp.cos(angle) / safe_sin)


def split(value):
    high = value.astype(BF16)
    return high, (value - high.astype(F32)).astype(BF16)


def mm(left, right):
    return jnp.dot(left, right, preferred_element_type=F32)


def mm_nt(left, right):
    return lax.dot_general(left, right, (((1,), (1,)), ((), ())), preferred_element_type=F32)


def kernel(
    n,
    seed_ref,
    inv_ref,
    w_in_ref,
    shapes_ref,
    gain_ref,
    faces_ref,
    g_ref,
    col_ref,
    send_ref,
    out_ref,
    part_ref,
    w_ref,
    gain_pad,
    left_hot,
    m_high,
    m_low,
    mg_high,
    mg_low,
    p_ref,
    sel_ref,
    x_ref,
    z_ref,
    base_ref,
    ab_ref,
    q_all,
    ghost_out,
    ghost_in,
    q_send,
    q_recv,
    g_send,
    g_recv,
):
    nvar, count, owned = seed_ref.shape
    modes = shapes_ref.shape[1]
    rows = count * nvar
    halo = send_ref.shape[1]
    nfaces = g_ref.shape[1]
    me = lax.axis_index("cell")
    peers = [lax.rem(me + d, n) for d in range(n)]

    barrier = pltpu.get_barrier_semaphore()
    for d in range(1, n):
        pl.semaphore_signal(barrier, inc=1, device_id={"cell": peers[d]}, device_id_type=pl.DeviceIdType.MESH)

    left = faces_ref[0:1, :]
    right = faces_ref[1:2, :]
    g_high, g_low = split(g_ref[...])
    one = jnp.ones((1, nfaces), BF16)
    step = 128
    tall = owned + halo

    def hot(index, start, size, value):
        lines = lax.broadcasted_iota(jnp.int32, (size, 128), 0).astype(jnp.int16)
        lines = jnp.concatenate([lines] * (nfaces // 128), axis=1)
        near = jnp.broadcast_to((index - start).astype(jnp.int16), (size, nfaces))
        zero = jnp.zeros((size, nfaces), BF16)
        return jnp.where(near == lines, jnp.broadcast_to(value, (size, nfaces)), zero)

    @pl.loop(0, tall // step)
    def _(t):
        at = pl.multiple_of(t * step, step)
        left_hot[0, pl.ds(at, step), :] = hot(left, at, step, g_high)
        left_hot[1, pl.ds(at, step), :] = hot(left, at, step, g_low)

    wide = 256
    tall_step = tall // 3

    @pl.loop(0, owned // wide)
    def _(t):
        at = pl.multiple_of(t * wide, wide)
        right_hot = hot(right, at, wide, one)
        for part in range(3):
            r0 = part * tall_step
            block = mm_nt(left_hot[0, r0 : r0 + tall_step, :], right_hot) + mm_nt(left_hot[1, r0 : r0 + tall_step, :], right_hot)
            high, low = split(block)
            here = min(r0 + tall_step, owned) - r0
            m_high[r0 : r0 + here, pl.ds(at, wide)] = high[:here]
            m_low[r0 : r0 + here, pl.ds(at, wide)] = low[:here]
            if here < tall_step:
                mg_high[0:halo, pl.ds(at, wide)] = high[here:]
                mg_low[0:halo, pl.ds(at, wide)] = low[here:]

    upper_high = hot(right, owned + halo, halo, g_high)
    upper_low = hot(right, owned + halo, halo, g_low)
    upper_hot = jnp.concatenate([upper_high, upper_low], axis=0)

    @pl.loop(0, owned // wide)
    def _(t):
        at = pl.multiple_of(t * wide, wide)
        block = mm_nt(upper_hot, hot(left, at, wide, one))
        high, low = split(block[:halo] + block[halo:])
        mg_high[halo:, pl.ds(at, wide)] = high
        mg_low[halo:, pl.ds(at, wide)] = low

    w_high, w_low = split(w_in_ref[...])
    lane = lax.broadcasted_iota(jnp.int32, (rows, 3 * rows), 1)
    line = lax.broadcasted_iota(jnp.int32, (rows, 3 * rows), 0)
    first = jnp.where((lane == line) | (lane == line + rows), 1.0, 0.0).astype(BF16)
    last = jnp.where(lane == line + 2 * rows, 1.0, 0.0).astype(BF16)
    w_ref[...] = (mm(w_high, first) + mm(w_low, last)).astype(BF16)
    gain_pad[...] = jnp.zeros((1, 128), F32)
    gain_pad[:, 0:modes] = gain_ref[...]
    send_row = jnp.concatenate([send_ref[0:1, :], send_ref[1:2, :]], axis=1)
    sel_ref[...] = jnp.where(
        send_row == lax.broadcasted_iota(jnp.int32, (owned, 2 * halo), 0), 1.0, 0.0
    ).astype(BF16)
    for v in range(nvar):
        shape_v = shapes_ref[v]
        shape_v = jnp.concatenate([shape_v, jnp.zeros((MODE_ROWS - modes, owned), F32)], axis=0)
        high, low = split(shape_v)
        p_ref[v, 0:MODE_ROWS, :] = high
        p_ref[v, MODE_ROWS:, :] = low
        z_ref[v * count : (v + 1) * count, :] = seed_ref[v]
    colours = col_ref[...]

    def update(colour):
        mask = colours == colour
        for w in range(nvar):
            spot = slice(w * count, (w + 1) * count)
            total = inv_ref[0, w].astype(F32) * z_ref[0:count, :]
            for v in range(1, nvar):
                total = total + inv_ref[v, w].astype(F32) * z_ref[v * count : (v + 1) * count, :]
            x_ref[spot, :] = jnp.where(mask, total, x_ref[spot, :])

    def coupling():
        high, low = split(x_ref[...])
        both = mm(w_ref[...], jnp.concatenate([high, low, high], axis=0))
        a_high, a_low = split(both[:rows])
        b_high, b_low = split(both[rows : 2 * rows])
        ab_ref[0, 0:rows, :] = a_high
        ab_ref[0, rows:, :] = a_low
        ab_ref[1, 0:rows, :] = b_high
        ab_ref[1, rows:, :] = b_low
        z_ref[...] = both[2 * rows :]

        @pl.loop(0, owned // wide)
        def _(t):
            at = pl.multiple_of(t * wide, wide)
            cols = pl.ds(at, wide)
            one = mm(ab_ref[0], m_high[:, cols]) + mm_nt(ab_ref[1], m_high[cols, :])
            two = mm(ab_ref[0, 0:rows, :], m_low[:, cols]) + mm_nt(ab_ref[1, 0:rows, :], m_low[cols, :])
            z_ref[:, cols] = z_ref[:, cols] + (one[:rows] + one[rows:] + two)

    def modal_copies(turn):
        return [
            pltpu.make_async_remote_copy(
                src_ref=q_all.at[turn, me],
                dst_ref=q_all.at[turn, me],
                send_sem=q_send.at[turn, d],
                recv_sem=q_recv.at[turn, d],
                device_id={"cell": peers[d]},
                device_id_type=pl.DeviceIdType.MESH,
            )
            for d in range(1, n)
        ]

    def ghost_copies(turn):
        return [
            pltpu.make_async_remote_copy(
                src_ref=ghost_out.at[turn, way],
                dst_ref=ghost_in.at[turn, 1 - way],
                send_sem=g_send.at[turn, way],
                recv_sem=g_recv.at[turn, way],
                device_id={"cell": peers[n - 1 if way == 0 else 1]},
                device_id_type=pl.DeviceIdType.MESH,
            )
            for way in range(2)
        ]

    def start_exchange(turn):
        high, low = split(x_ref[...])
        copies = []
        if turn < ITERS - 1:
            picked = mm(jnp.concatenate([high, low], axis=0), sel_ref[...])
            picked = picked[:rows] + picked[rows:]
            ghost_out[turn, 0] = picked[:, :halo]
            ghost_out[turn, 1] = picked[:, halo:]
            copies = ghost_copies(turn)
            if turn == 0:
                pl.semaphore_wait(barrier, n - 1)
            for copy in copies:
                copy.start()
        gram = jnp.zeros((2 * count, 2 * MODE_ROWS), F32)
        for v in range(nvar):
            spot = slice(v * count, (v + 1) * count)
            gram = gram + mm_nt(jnp.concatenate([high[spot], low[spot]], axis=0), p_ref[v])
        gram = gram[:count] + gram[count:]
        part = gram[:, :MODE_ROWS] + gram[:, MODE_ROWS:]
        q_all[turn, me] = jnp.concatenate([part, jnp.zeros((count, 128 - MODE_ROWS), F32)], axis=1)
        modal = modal_copies(turn)
        for copy in modal:
            copy.start()
        return copies + modal

    def modal_sum(turn):
        total = q_all[turn, 0]
        for d in range(1, n):
            total = total + q_all[turn, d]
        return total

    x_ref[...] = jnp.zeros((rows, owned), F32)
    update(0)
    coupling()
    for v in range(nvar):
        spot = slice(v * count, (v + 1) * count)
        z_ref[spot, :] = seed_ref[v] - z_ref[spot, :]
    update(1)
    copies = start_exchange(0)
    for sweep in range(1, ITERS):
        coupling()
        for copy in copies:
            copy.wait()
        low_part = ghost_in[sweep - 1, 0]
        up_part = ghost_in[sweep - 1, 1]
        high, low = split(jnp.concatenate([low_part, up_part], axis=1))
        both = mm(w_ref[0 : 2 * rows, :], jnp.concatenate([high, low, high], axis=0))
        ghost_ab = jnp.concatenate([both[:rows, :halo], both[rows:, halo:]], axis=1)
        high, low = split(ghost_ab)
        term = mm(jnp.concatenate([high, low], axis=0), mg_high[...])
        term = term[:rows] + term[rows:] + mm(high, mg_low[...])
        lam = modal_sum(sweep - 1)[:, :MODE_ROWS] * gain_pad[:, :MODE_ROWS]
        lam_high, lam_low = split(lam)
        lam_both = jnp.concatenate([lam_high, lam_low], axis=0)
        for v in range(nvar):
            spot = slice(v * count, (v + 1) * count)
            lift = mm(lam_both, p_ref[v, 0:MODE_ROWS, :])
            lift = lift[:count] + lift[count:] + mm(lam_high, p_ref[v, MODE_ROWS:, :])
            base = seed_ref[v] + lift - term[spot]
            base_ref[spot, :] = base
            z_ref[spot, :] = base - z_ref[spot, :]
        update(0)
        coupling()
        z_ref[...] = base_ref[...] - z_ref[...]
        update(1)
        copies = start_exchange(sweep)
    for v in range(nvar):
        out_ref[v] = x_ref[v * count : (v + 1) * count, :]
    for copy in copies:
        copy.wait()
    part_ref[...] = modal_sum(ITERS - 1)[:, :modes]


def local(
    adjoint_seed,
    inv_blocks,
    flux_jacobians,
    modal_shapes,
    modal_gain,
    face_cells,
    face_weights,
    colours,
    send_cells,
):
    n = lax.axis_size("cell")
    count, nvar, owned = adjoint_seed.shape
    modes = modal_shapes.shape[0]
    rows = count * nvar
    halo = send_cells.shape[1]
    nfaces = face_weights.shape[0]
    eye_inst = jnp.eye(count, dtype=F32)
    eye_var = jnp.eye(nvar, dtype=F32)
    left_matrix = (
        jnp.transpose(flux_jacobians[0], (2, 0, 1))[:, :, :, None] * eye_inst[None, :, None, :]
    ).reshape(rows, rows)
    right_matrix = (
        jnp.transpose(flux_jacobians[1], (2, 0, 1))[:, :, :, None] * eye_inst[None, :, None, :]
    ).reshape(rows, rows)
    spectral = FREQUENCY * spectral_matrix(count)
    spectral_rows = (eye_var[:, None, :, None] * spectral.T[None, :, None, :]).reshape(rows, rows)
    stacked = jnp.concatenate([left_matrix, right_matrix, spectral_rows], axis=0)
    inverse = jnp.transpose(inv_blocks, (1, 2, 0, 3))
    vmem = pl.BlockSpec(memory_space=pltpu.VMEM)
    tall = owned + halo
    turns = ITERS
    out, part = pl.pallas_call(
        functools.partial(kernel, n),
        out_shape=(
            jax.ShapeDtypeStruct((nvar, count, owned), F32),
            jax.ShapeDtypeStruct((count, modes), F32),
        ),
        in_specs=[vmem] * 9,
        out_specs=(vmem, vmem),
        scratch_shapes=[
            pltpu.VMEM((3 * rows, 3 * rows), BF16),
            pltpu.VMEM((1, 128), F32),
            pltpu.VMEM((2, tall, nfaces), BF16),
            pltpu.VMEM((owned, owned), BF16),
            pltpu.VMEM((owned, owned), BF16),
            pltpu.VMEM((2 * halo, owned), BF16),
            pltpu.VMEM((2 * halo, owned), BF16),
            pltpu.VMEM((nvar, 2 * MODE_ROWS, owned), BF16),
            pltpu.VMEM((owned, 2 * halo), BF16),
            pltpu.VMEM((rows, owned), F32),
            pltpu.VMEM((rows, owned), F32),
            pltpu.VMEM((rows, owned), F32),
            pltpu.VMEM((2, 2 * rows, owned), BF16),
            pltpu.VMEM((turns, n, count, 128), F32),
            pltpu.VMEM((turns - 1, 2, rows, halo), F32),
            pltpu.VMEM((turns - 1, 2, rows, halo), F32),
            pltpu.SemaphoreType.DMA((turns, n)),
            pltpu.SemaphoreType.DMA((turns, n)),
            pltpu.SemaphoreType.DMA((turns - 1, 2)),
            pltpu.SemaphoreType.DMA((turns - 1, 2)),
        ],
        compiler_params=pltpu.CompilerParams(
            collective_id=0, has_side_effects=True, vmem_limit_bytes=56 * 1024 * 1024
        ),
    )(
        jnp.transpose(adjoint_seed, (1, 0, 2)),
        inverse,
        stacked,
        jnp.transpose(modal_shapes, (1, 0, 2)),
        modal_gain[None, :],
        face_cells,
        face_weights[None, :],
        colours[None, :],
        send_cells,
    )
    return jnp.transpose(out, (1, 0, 2)), part


def solution(mesh):
    return jax.shard_map(
        local,
        mesh=mesh,
        in_specs=(
            P("group", None, "cell"),
            P("group", None, None, "cell"),
            P(None, "group", None, None),
            P(None, None, "cell"),
            P("group"),
            P(None, "cell"),
            P("cell"),
            P("cell"),
            P(None, "cell"),
        ),
        out_specs=(P("group", None, "cell"), P("group", None)),
        check_vma=False,
    )
```

```python
import functools
import math

import jax
import jax.numpy as jnp
from jax import lax
from jax.experimental import pallas as pl
from jax.experimental.pallas import tpu as pltpu
from jax.sharding import PartitionSpec as P

ITERS = 4
FREQUENCY = 0.04
F32 = jnp.float32
BF16 = jnp.bfloat16
F8 = jnp.float8_e4m3fn
LIFT = 256.0
MODE_ROWS = 32


def spectral_matrix(count):
    index = jnp.arange(count)
    apart = index[:, None] - index[None, :]
    angle = math.pi * apart.astype(F32) / count
    parity = jnp.where(apart % 2 == 0, 1.0, -1.0).astype(F32)
    safe_sin = jnp.where(apart == 0, 1.0, jnp.sin(angle))
    return jnp.where(apart == 0, 0.0, 0.5 * parity * jnp.cos(angle) / safe_sin)


def split(value):
    high = value.astype(BF16)
    return high, (value - high.astype(F32)).astype(BF16)


def mm(left, right):
    return jnp.dot(left, right, preferred_element_type=F32)


def mm_nt(left, right):
    return lax.dot_general(left, right, (((1,), (1,)), ((), ())), preferred_element_type=F32)


def kernel(
    n,
    seed_ref,
    inv_ref,
    w_in_ref,
    shapes_ref,
    gain_ref,
    faces_ref,
    g_ref,
    col_ref,
    send_ref,
    out_ref,
    part_ref,
    w_ref,
    gain_pad,
    left_hot,
    left_low,
    m_high,
    m_low,
    mg_high,
    mg_low,
    p_ref,
    sel_ref,
    x_ref,
    z_ref,
    base_ref,
    ab_ref,
    q_all,
    ghost_out,
    ghost_in,
    q_send,
    q_recv,
    g_send,
    g_recv,
):
    nvar, count, owned = seed_ref.shape
    modes = shapes_ref.shape[1]
    rows = count * nvar
    halo = send_ref.shape[1]
    nfaces = g_ref.shape[1]
    me = lax.axis_index("cell")
    peers = [lax.rem(me + d, n) for d in range(n)]

    barrier = pltpu.get_barrier_semaphore()
    for d in range(1, n):
        pl.semaphore_signal(barrier, inc=1, device_id={"cell": peers[d]}, device_id_type=pl.DeviceIdType.MESH)

    left = faces_ref[0:1, :]
    right = faces_ref[1:2, :]
    g_high, g_low = split(g_ref[...])
    one = jnp.ones((1, nfaces), BF16)
    step = 128
    tall = owned + halo

    def hot(index, start, size, value):
        lines = lax.broadcasted_iota(jnp.int32, (size, 128), 0).astype(jnp.int16)
        lines = jnp.concatenate([lines] * (nfaces // 128), axis=1)
        near = jnp.broadcast_to((index - start).astype(jnp.int16), (size, nfaces))
        zero = jnp.zeros((size, nfaces), BF16)
        return jnp.where(near == lines, jnp.broadcast_to(value, (size, nfaces)), zero)

    @pl.loop(0, tall // step)
    def _(t):
        at = pl.multiple_of(t * step, step)
        left_hot[pl.ds(at, step), :] = hot(left, at, step, g_high)
        left_low[pl.ds(at, step), :] = (hot(left, at, step, g_low).astype(F32) * LIFT).astype(F8)

    wide = 256
    tall_step = tall // 3

    @pl.loop(0, owned // wide)
    def _(t):
        at = pl.multiple_of(t * wide, wide)
        right_hot = hot(right, at, wide, one)
        right_low = right_hot.astype(F32).astype(F8)
        for part in range(3):
            r0 = part * tall_step
            block = mm_nt(left_hot[r0 : r0 + tall_step, :], right_hot)
            block = block + mm_nt(left_low[r0 : r0 + tall_step, :], right_low) * (1.0 / LIFT)
            high, low = split(block)
            here = min(r0 + tall_step, owned) - r0
            m_high[r0 : r0 + here, pl.ds(at, wide)] = high[:here]
            m_low[r0 : r0 + here, pl.ds(at, wide)] = low[:here]
            if here < tall_step:
                mg_high[0:halo, pl.ds(at, wide)] = high[here:]
                mg_low[0:halo, pl.ds(at, wide)] = low[here:]

    upper_high = hot(right, owned + halo, halo, g_high)
    upper_low = hot(right, owned + halo, halo, g_low)
    upper_hot = jnp.concatenate([upper_high, upper_low], axis=0)

    @pl.loop(0, owned // wide)
    def _(t):
        at = pl.multiple_of(t * wide, wide)
        block = mm_nt(upper_hot, hot(left, at, wide, one))
        high, low = split(block[:halo] + block[halo:])
        mg_high[halo:, pl.ds(at, wide)] = high
        mg_low[halo:, pl.ds(at, wide)] = low

    w_high, w_low = split(w_in_ref[...])
    lane = lax.broadcasted_iota(jnp.int32, (rows, 3 * rows), 1)
    line = lax.broadcasted_iota(jnp.int32, (rows, 3 * rows), 0)
    first = jnp.where((lane == line) | (lane == line + rows), 1.0, 0.0).astype(BF16)
    last = jnp.where(lane == line + 2 * rows, 1.0, 0.0).astype(BF16)
    w_ref[...] = (mm(w_high, first) + mm(w_low, last)).astype(BF16)
    gain_pad[...] = jnp.zeros((1, 128), F32)
    gain_pad[:, 0:modes] = gain_ref[...]
    send_row = jnp.concatenate([send_ref[0:1, :], send_ref[1:2, :]], axis=1)
    sel_ref[...] = jnp.where(
        send_row == lax.broadcasted_iota(jnp.int32, (owned, 2 * halo), 0), 1.0, 0.0
    ).astype(BF16)
    for v in range(nvar):
        shape_v = shapes_ref[v]
        shape_v = jnp.concatenate([shape_v, jnp.zeros((MODE_ROWS - modes, owned), F32)], axis=0)
        high, low = split(shape_v)
        p_ref[v, 0:MODE_ROWS, :] = high
        p_ref[v, MODE_ROWS:, :] = low
        z_ref[v * count : (v + 1) * count, :] = seed_ref[v]
    colours = col_ref[...]

    def update(colour):
        mask = colours == colour
        for w in range(nvar):
            spot = slice(w * count, (w + 1) * count)
            total = inv_ref[0, w].astype(F32) * z_ref[0:count, :]
            for v in range(1, nvar):
                total = total + inv_ref[v, w].astype(F32) * z_ref[v * count : (v + 1) * count, :]
            x_ref[spot, :] = jnp.where(mask, total, x_ref[spot, :])

    def coupling():
        high, low = split(x_ref[...])
        both = mm(w_ref[...], jnp.concatenate([high, low, high], axis=0))
        a_high, a_low = split(both[:rows])
        b_high, b_low = split(both[rows : 2 * rows])
        ab_ref[0, 0:rows, :] = a_high
        ab_ref[0, rows:, :] = a_low
        ab_ref[1, 0:rows, :] = b_high
        ab_ref[1, rows:, :] = b_low
        z_ref[...] = both[2 * rows :]

        @pl.loop(0, owned // wide)
        def _(t):
            at = pl.multiple_of(t * wide, wide)
            cols = pl.ds(at, wide)
            one = mm(ab_ref[0], m_high[:, cols]) + mm_nt(ab_ref[1], m_high[cols, :])
            two = mm(ab_ref[0, 0:rows, :], m_low[:, cols]) + mm_nt(ab_ref[1, 0:rows, :], m_low[cols, :])
            z_ref[:, cols] = z_ref[:, cols] + (one[:rows] + one[rows:] + two)

    def modal_copies(turn):
        return [
            pltpu.make_async_remote_copy(
                src_ref=q_all.at[turn, me],
                dst_ref=q_all.at[turn, me],
                send_sem=q_send.at[turn, d],
                recv_sem=q_recv.at[turn, d],
                device_id={"cell": peers[d]},
                device_id_type=pl.DeviceIdType.MESH,
            )
            for d in range(1, n)
        ]

    def ghost_copies(turn):
        return [
            pltpu.make_async_remote_copy(
                src_ref=ghost_out.at[turn, way],
                dst_ref=ghost_in.at[turn, 1 - way],
                send_sem=g_send.at[turn, way],
                recv_sem=g_recv.at[turn, way],
                device_id={"cell": peers[n - 1 if way == 0 else 1]},
                device_id_type=pl.DeviceIdType.MESH,
            )
            for way in range(2)
        ]

    def start_exchange(turn):
        high, low = split(x_ref[...])
        copies = []
        if turn < ITERS - 1:
            picked = mm(jnp.concatenate([high, low], axis=0), sel_ref[...])
            picked = picked[:rows] + picked[rows:]
            ghost_out[turn, 0] = picked[:, :halo]
            ghost_out[turn, 1] = picked[:, halo:]
            copies = ghost_copies(turn)
            if turn == 0:
                pl.semaphore_wait(barrier, n - 1)
            for copy in copies:
                copy.start()
        gram = jnp.zeros((2 * count, 2 * MODE_ROWS), F32)
        for v in range(nvar):
            spot = slice(v * count, (v + 1) * count)
            gram = gram + mm_nt(jnp.concatenate([high[spot], low[spot]], axis=0), p_ref[v])
        gram = gram[:count] + gram[count:]
        part = gram[:, :MODE_ROWS] + gram[:, MODE_ROWS:]
        half = count // 2
        q_all[turn, me] = jnp.concatenate(
            [part[:half], part[half:], jnp.zeros((half, 128 - 2 * MODE_ROWS), F32)], axis=1
        )
        modal = modal_copies(turn)
        for copy in modal:
            copy.start()
        return copies + modal

    def modal_sum(turn):
        total = q_all[turn, 0]
        for d in range(1, n):
            total = total + q_all[turn, d]
        return jnp.concatenate([total[:, :MODE_ROWS], total[:, MODE_ROWS : 2 * MODE_ROWS]], axis=0)

    x_ref[...] = jnp.zeros((rows, owned), F32)
    update(0)
    coupling()
    for v in range(nvar):
        spot = slice(v * count, (v + 1) * count)
        z_ref[spot, :] = seed_ref[v] - z_ref[spot, :]
    update(1)
    copies = start_exchange(0)
    for sweep in range(1, ITERS):
        coupling()
        for copy in copies:
            copy.wait()
        low_part = ghost_in[sweep - 1, 0]
        up_part = ghost_in[sweep - 1, 1]
        high, low = split(jnp.concatenate([low_part, up_part], axis=1))
        both = mm(w_ref[0 : 2 * rows, :], jnp.concatenate([high, low, high], axis=0))
        ghost_ab = jnp.concatenate([both[:rows, :halo], both[rows:, halo:]], axis=1)
        high, low = split(ghost_ab)
        term = mm(jnp.concatenate([high, low], axis=0), mg_high[...])
        term = term[:rows] + term[rows:] + mm(high, mg_low[...])
        lam = modal_sum(sweep - 1)[:, :MODE_ROWS] * gain_pad[:, :MODE_ROWS]
        lam_high, lam_low = split(lam)
        lam_both = jnp.concatenate([lam_high, lam_low], axis=0)
        for v in range(nvar):
            spot = slice(v * count, (v + 1) * count)
            lift = mm(lam_both, p_ref[v, 0:MODE_ROWS, :])
            lift = lift[:count] + lift[count:] + mm(lam_high, p_ref[v, MODE_ROWS:, :])
            base = seed_ref[v] + lift - term[spot]
            base_ref[spot, :] = base
            z_ref[spot, :] = base - z_ref[spot, :]
        update(0)
        coupling()
        z_ref[...] = base_ref[...] - z_ref[...]
        update(1)
        copies = start_exchange(sweep)
    for v in range(nvar):
        out_ref[v] = x_ref[v * count : (v + 1) * count, :]
    for copy in copies:
        copy.wait()
    part_ref[...] = modal_sum(ITERS - 1)[:, :modes]


def local(
    adjoint_seed,
    inv_blocks,
    flux_jacobians,
    modal_shapes,
    modal_gain,
    face_cells,
    face_weights,
    colours,
    send_cells,
):
    n = lax.axis_size("cell")
    count, nvar, owned = adjoint_seed.shape
    modes = modal_shapes.shape[0]
    rows = count * nvar
    halo = send_cells.shape[1]
    nfaces = face_weights.shape[0]
    eye_inst = jnp.eye(count, dtype=F32)
    eye_var = jnp.eye(nvar, dtype=F32)
    left_matrix = (
        jnp.transpose(flux_jacobians[0], (2, 0, 1))[:, :, :, None] * eye_inst[None, :, None, :]
    ).reshape(rows, rows)
    right_matrix = (
        jnp.transpose(flux_jacobians[1], (2, 0, 1))[:, :, :, None] * eye_inst[None, :, None, :]
    ).reshape(rows, rows)
    spectral = FREQUENCY * spectral_matrix(count)
    spectral_rows = (eye_var[:, None, :, None] * spectral.T[None, :, None, :]).reshape(rows, rows)
    stacked = jnp.concatenate([left_matrix, right_matrix, spectral_rows], axis=0)
    inverse = jnp.transpose(inv_blocks, (1, 2, 0, 3))
    vmem = pl.BlockSpec(memory_space=pltpu.VMEM)
    tall = owned + halo
    turns = ITERS
    out, part = pl.pallas_call(
        functools.partial(kernel, n),
        out_shape=(
            jax.ShapeDtypeStruct((nvar, count, owned), F32),
            jax.ShapeDtypeStruct((count, modes), F32),
        ),
        in_specs=[vmem] * 9,
        out_specs=(vmem, vmem),
        scratch_shapes=[
            pltpu.VMEM((3 * rows, 3 * rows), BF16),
            pltpu.VMEM((1, 128), F32),
            pltpu.VMEM((tall, nfaces), BF16),
            pltpu.VMEM((tall, nfaces), F8),
            pltpu.VMEM((owned, owned), BF16),
            pltpu.VMEM((owned, owned), BF16),
            pltpu.VMEM((2 * halo, owned), BF16),
            pltpu.VMEM((2 * halo, owned), BF16),
            pltpu.VMEM((nvar, 2 * MODE_ROWS, owned), BF16),
            pltpu.VMEM((owned, 2 * halo), BF16),
            pltpu.VMEM((rows, owned), F32),
            pltpu.VMEM((rows, owned), F32),
            pltpu.VMEM((rows, owned), F32),
            pltpu.VMEM((2, 2 * rows, owned), BF16),
            pltpu.VMEM((turns, n, count // 2, 128), F32),
            pltpu.VMEM((turns - 1, 2, rows, halo), F32),
            pltpu.VMEM((turns - 1, 2, rows, halo), F32),
            pltpu.SemaphoreType.DMA((turns, n)),
            pltpu.SemaphoreType.DMA((turns, n)),
            pltpu.SemaphoreType.DMA((turns - 1, 2)),
            pltpu.SemaphoreType.DMA((turns - 1, 2)),
        ],
        compiler_params=pltpu.CompilerParams(
            collective_id=0, has_side_effects=True, vmem_limit_bytes=56 * 1024 * 1024
        ),
    )(
        jnp.transpose(adjoint_seed, (1, 0, 2)),
        inverse,
        stacked,
        jnp.transpose(modal_shapes, (1, 0, 2)),
        modal_gain[None, :],
        face_cells,
        face_weights[None, :],
        colours[None, :],
        send_cells,
    )
    return jnp.transpose(out, (1, 0, 2)), part


def solution(mesh):
    return jax.shard_map(
        local,
        mesh=mesh,
        in_specs=(
            P("group", None, "cell"),
            P("group", None, None, "cell"),
            P(None, "group", None, None),
            P(None, None, "cell"),
            P("group"),
            P(None, "cell"),
            P("cell"),
            P("cell"),
            P(None, "cell"),
        ),
        out_specs=(P("group", None, "cell"), P("group", None)),
        check_vma=False,
    )
```
